32 devices in a mesh: dict: 4 (over y, x), dp: 8 (over z, core).
Axes of the slice: x: 2, y: 2, z: 4, core: 2. Of those that a mesh axis runs over, the one named last changes fastest.
Arguments:
- activations: bfloat16 [2048, 3584], P('dp', 'dict'), may hold values from -6 to 6
- dictionary: bfloat16 [32768, 3584], P(('dict', 'dp')), may hold values from -0.09375 to 0.09375
- enc_bias: bfloat16 [32768], P(('dict', 'dp')), may hold values from -1.5 to 0
- dec_bias: float32 [3584], replicated, may hold values from -3 to 3
- block_codes: int32 [16, 4, 8], P('dp'), may hold values from -1 to 255, as said below
Outputs:
- error: bfloat16 [2048, 3584], P('dp', 'dict')
- grad_dict: float32 [32768, 3584], P(('dict', 'dp'))
- grad_enc_bias: float32 [32768], P(('dict', 'dp'))
The draws below stay inside these ranges and needn't reach their ends.
Inputs may be any that keep to these rules, and one draw needn't show every extreme that they name: `block_codes`: entry [b, s, m] is either -1 (an empty slot) or a latent block of shard s, that is one of the blocks s * 64 upward. Block k is held by the dp index (k % 64) // 8. Every token block names exactly 32 blocks in all and at most 8 in one shard, reached in every draw; within one shard its blocks are held by distinct dp indices. All token blocks of one dp index that name a block held by the same dp index of the same shard name the same block.
All inputs are finite; a program needn't handle non-finite values.
Results may differ from the reference program's by a relative error of at most 0.012.
The reference program's roundings to bfloat16 on the way count: a program that leaves them out, or rounds other values in their place, can miss the bound.
Values may be sent and summed in bfloat16 or wider, within the bound.
No kernel may reach another device: no remote copies, remote signals or barrier semaphores. Data moves between devices by JAX's collectives and lax.ppermute only.
A program may use at most 128 MiB of HBM per device.

```python
import jax
import jax.numpy as jnp
from jax import lax

D = 3584
LAT_DICT = 8192
DICT_SPAN = 128
SAMPLE_SPAN = 128
ACT_S = 8
SAMPLES_REPLICA = 256
LAT = 32768
SWING = 0
MOST = 8
TOKENS = 2048
NBLK = 16
NTB = 2
N_DICT = 4
N_DP = 8


def draw_block_codes(key, part):
    key_pick, key_order, key_shift, key_owner = jax.random.split(key, 4)
    shard_blocks = LAT_DICT // DICT_SPAN
    own_blocks = shard_blocks // N_DP
    per_group = SAMPLES_REPLICA // SAMPLE_SPAN
    choose = jax.random.randint(key_pick, (N_DP, N_DICT, N_DP), 0, own_blocks, dtype=jnp.int32)
    ranking_scores = jax.random.randint(key_order, (NBLK, N_DICT), 0, 1 << 20, dtype=jnp.int32) * N_DICT + jnp.arange(N_DICT, dtype=jnp.int32)
    shard_order = jnp.argsort(ranking_scores, axis=1, stable=True).astype(jnp.int32)
    pair_count = N_DICT // 2
    shifts = jax.random.randint(key_shift, (NBLK, pair_count), -SWING, SWING + 1, dtype=jnp.int32)
    leading = jnp.arange(NBLK, dtype=jnp.int32) % per_group == 0
    shifts = shifts.at[:, 0].set(jnp.where(leading, SWING, shifts[:, 0]))
    signed = jnp.stack([shifts, -shifts], axis=2).reshape(NBLK, N_DICT)
    onehot = (shard_order[:, :, None] == jnp.arange(N_DICT, dtype=jnp.int32)).astype(jnp.int32)
    counts = ACT_S + jnp.sum(onehot * signed[:, :, None], axis=1)
    owner_scores = jax.random.randint(key_owner, (NBLK, N_DICT, N_DP), 0, 1 << 20, dtype=jnp.int32) * N_DP + jnp.arange(N_DP, dtype=jnp.int32)
    _, owners = lax.top_k(owner_scores, MOST)
    group_of = jnp.arange(NBLK, dtype=jnp.int32) // per_group
    inner_pick = jnp.take_along_axis(choose[group_of], owners, axis=2)
    block_ids = jnp.arange(N_DICT, dtype=jnp.int32)[None, :, None] * shard_blocks + owners * own_blocks + inner_pick
    slot_pos = jnp.arange(MOST, dtype=jnp.int32)[None, None, :]
    return jnp.where(slot_pos < counts[:, :, None], block_ids, -1).astype(jnp.int32)


def block_scale(stream_key, dims, pieces, smallest, high):
    gain = 1.0
    for position, parts in pieces:
        steps = jax.random.uniform(jax.random.fold_in(jax.random.fold_in(stream_key, 6), position), (parts,), jnp.float32, smallest / len(pieces), high / len(pieces))
        gain = gain * jnp.repeat(jnp.exp(steps), dims[position] // parts).reshape((-1,) + (1,) * (len(dims) - 1 - position))
    return gain


def noise(stream_key, dims, scale, reach, pieces=(), kind=jnp.bfloat16):
    level = block_scale(stream_key, dims, pieces, -0.22, 0.18) if pieces else 1.0
    entries = jax.random.normal(stream_key, dims, jnp.float32) * scale * level
    return jnp.minimum(jnp.maximum(entries, -reach), reach).astype(kind)


def setup_inputs(seed: int = 0) -> dict:
    keys = jax.random.split(jax.random.key(seed), 6)
    activations = noise(keys[0], (TOKENS, D), 1.0, 6.0, ((0, 8), (1, 4)))
    dictionary = noise(keys[1], (LAT, D), D ** -0.5, 0.09375, ((0, 32),))
    enc_bias = jnp.clip(-1.5 + 1.5 * jax.random.uniform(keys[2], (LAT,), jnp.float32) ** block_scale(keys[2], (LAT,), ((0, 32),), -0.2, 0.2), -1.5, 0.0).astype(jnp.bfloat16)
    dec_bias = noise(keys[3], (D,), 0.5, 3.0, (), jnp.float32)
    block_codes = draw_block_codes(jax.random.fold_in(keys[5], 71), 0)
    return dict(activations=activations, dictionary=dictionary, enc_bias=enc_bias, dec_bias=dec_bias, block_codes=block_codes)


def reference(activations, dictionary, enc_bias, dec_bias, block_codes):
    shard_blocks = LAT_DICT // DICT_SPAN
    own_blocks = shard_blocks // N_DP
    all_blocks = LAT // DICT_SPAN
    position_total = N_DICT * N_DP
    slot_rows = position_total * DICT_SPAN
    table_w = dictionary.reshape(all_blocks, DICT_SPAN, D)
    table_b = enc_bias.reshape(all_blocks, DICT_SPAN)
    shard_ids = jnp.arange(N_DICT, dtype=jnp.int32)[None, :, None]
    peer_ids = jnp.arange(N_DP, dtype=jnp.int32)

    def group_step(carry, inputs):
        grad_w, grad_b = carry
        tokens, group_codes = inputs
        filled = group_codes >= 0
        owning = jnp.where(filled, (group_codes - shard_ids * shard_blocks) // own_blocks, -1)
        matches = owning[..., None] == peer_ids
        picked = jnp.max(jnp.where(matches, group_codes[..., None], -1), axis=(0, 2)).reshape(position_total)
        selected_entries = jnp.any(matches, axis=2).reshape(group_codes.shape[0], position_total)
        safe_ids = jnp.maximum(picked, 0).astype(jnp.int32)
        fetched = table_w[safe_ids].reshape(slot_rows, D)
        bias_flat = table_b[safe_ids].reshape(slot_rows).astype(jnp.float32)
        mean_removed = (tokens.astype(jnp.float32) - dec_bias).astype(jnp.bfloat16)
        preact = lax.dot_general(mean_removed, fetched, (((1,), (1,)), ((), ())), preferred_element_type=jnp.float32) + bias_flat
        encoder_input_tiles = preact.reshape(SAMPLES_REPLICA, position_total, DICT_SPAN)
        nonzero_indicator = jnp.repeat(selected_entries, SAMPLE_SPAN, axis=0)[:, :, None]
        hidden_activity = jnp.where(nonzero_indicator, jnp.maximum(encoder_input_tiles, 0.0), 0.0).astype(jnp.bfloat16)
        recon = jnp.dot(hidden_activity.reshape(SAMPLES_REPLICA, slot_rows), fetched, preferred_element_type=jnp.float32) + dec_bias
        error = (recon - tokens.astype(jnp.float32)).astype(jnp.bfloat16)
        returned_entries = lax.dot_general(error, fetched, (((1,), (1,)), ((), ())), preferred_element_type=jnp.float32)
        derivative_factor = jnp.where(nonzero_indicator & (encoder_input_tiles > 0), returned_entries.reshape(SAMPLES_REPLICA, position_total, DICT_SPAN), 0.0).astype(jnp.bfloat16)
        weight_summands = jnp.einsum("eaw,ep->awp", hidden_activity.astype(jnp.float32), error.astype(jnp.float32))
        weight_summands = weight_summands + jnp.einsum("eaw,ep->awp", derivative_factor.astype(jnp.float32), mean_removed.astype(jnp.float32))
        weight_summands = weight_summands.astype(jnp.bfloat16)
        terms_b = jnp.sum(derivative_factor.astype(jnp.float32), axis=0).astype(jnp.bfloat16)
        grad_w = grad_w.at[safe_ids].add(weight_summands.astype(jnp.float32))
        grad_b = grad_b.at[safe_ids].add(terms_b.astype(jnp.float32))
        return (grad_w, grad_b), error

    zeros_w = jnp.zeros((all_blocks, DICT_SPAN, D), jnp.float32)
    zeros_b = jnp.zeros((all_blocks, DICT_SPAN), jnp.float32)
    inputs = (activations.reshape(N_DP, SAMPLES_REPLICA, D), block_codes.reshape(N_DP, NTB, N_DICT, MOST))
    (grad_w, grad_b), errors = lax.scan(group_step, (zeros_w, zeros_b), inputs)
    return errors.reshape(TOKENS, D), grad_w.reshape(LAT, D), grad_b.reshape(LAT)
```

```python
import functools

import jax
import jax.numpy as jnp
from jax import lax
from jax.experimental import pallas as pl
from jax.experimental.pallas import tpu as pltpu
from jax.sharding import PartitionSpec as P

SPAN = 128
EXTRA = 16
VMEM_LIMIT = 48 * 1024 * 1024
BF = jnp.bfloat16
F32 = jnp.float32


def bits_of(slot):
    return [1 << b for b in range(slot.bit_length()) if slot >> b & 1]


def hop_bit(slot, half):
    bits = bits_of(slot)
    return bits[-1] if half == 0 else bits[0]


def over_dict(x, bit):
    n = lax.axis_size("dict")
    return lax.ppermute(x, "dict", [(i, i ^ bit) for i in range(n)])


def to_sibling(x):
    n = lax.axis_size("dp")
    return lax.ppermute(x, "dp", [(i, i ^ 1) for i in range(n)])


def along_ring(x):
    n = lax.axis_size("dp")
    return lax.ppermute(x, "dp", [(i, (i + 2) % n) for i in range(n)])


def gather_slots(own):
    n = lax.axis_size("dict")
    half = own.shape[0] // 2
    slots = {0: [own]}

    def rows(slot, h):
        pieces = slots[slot]
        if len(pieces) == 2:
            return pieces[h]
        return pieces[0][h * half : (h + 1) * half]

    for count in range(1, n.bit_length()):
        for slot in range(1, n):
            if slot.bit_count() != count:
                continue
            if count == 1:
                slots[slot] = [over_dict(own, slot)]
            else:
                slots[slot] = [
                    over_dict(rows(slot ^ hop_bit(slot, h), h), hop_bit(slot, h)) for h in (0, 1)
                ]
    return [slots[j] for j in range(n)]


def scatter_sum(parts):
    n = lax.axis_size("dict")
    acc = [list(p) for p in parts]
    for count in range(n.bit_length() - 1, 0, -1):
        moved = []
        for slot in range(1, n):
            if slot.bit_count() != count:
                continue
            for h in (0, 1):
                bit = hop_bit(slot, h)
                moved.append((slot ^ bit, h, over_dict(acc[slot][h].astype(BF), bit)))
        for slot, h, got in moved:
            acc[slot][h] = acc[slot][h].astype(F32) + got.astype(F32)
    return jnp.concatenate(acc[0], axis=0)


def nt_dot(a, b):
    return lax.dot_general(a, b, (((1,), (1,)), ((), ())), preferred_element_type=F32)


def fill_weights(w_refs, w_cat, fw):
    ns = len(w_refs) // 2
    for part in range(2):
        for j in range(ns):
            w_cat[part * SPAN : (part + 1) * SPAN, j * fw : (j + 1) * fw] = w_refs[part * ns + j][0]


def fill_rows(refs, layout, dst, fw, dec=None):
    for ref, (slot, row, count) in zip(refs, layout):
        cols = slice(slot * fw, (slot + 1) * fw)
        value = ref[...]
        if dec is not None:
            value = (value.astype(F32) - dec[:, cols]).astype(BF)
        dst[row : row + count, cols] = value


def fwd_kernel(layout, ns, fw, out_layout, meta, *refs):
    nx = len(layout)
    x_refs, refs = refs[:nx], refs[nx:]
    w_refs, refs = refs[: 2 * ns], refs[2 * ns :]
    dec, bias = refs[:2]
    lat_out = refs[2]
    outs = refs[3 : 3 + len(out_layout)]
    xc, wc = refs[3 + len(out_layout) :]
    fill_weights(w_refs, wc, fw)
    fill_rows(x_refs, layout, xc, fw, dec)
    preact = nt_dot(xc[...], wc[...]) + bias[...]
    tokens = preact.shape[0]
    for tb in range(tokens // SPAN):
        for part in range(2):
            cell = (slice(tb * SPAN, (tb + 1) * SPAN), slice(part * SPAN, (part + 1) * SPAN))
            named = jnp.full((SPAN, SPAN), meta[2 + 2 * tb + part], jnp.int32) > 0
            lat_out[cell] = jnp.where(named, jnp.maximum(preact[cell], 0.0), 0.0).astype(BF)
    lat = lat_out[...]
    for j in range(ns):
        recon = jnp.dot(lat, wc[:, j * fw : (j + 1) * fw], preferred_element_type=F32)
        for out, (slot, row, count) in zip(outs, out_layout):
            if slot == j:
                out[...] = recon[row : row + count].astype(out.dtype)


def bwd_kernel(x_layout, e_layout, ns, fw, meta, *refs):
    nx, ne = len(x_layout), len(e_layout)
    x_refs, refs = refs[:nx], refs[nx:]
    e_refs, refs = refs[:ne], refs[ne:]
    w_refs, refs = refs[: 2 * ns], refs[2 * ns :]
    dec, lat_ref, own_out, sib_out, xc, ec, wc = refs
    fill_weights(w_refs, wc, fw)
    fill_rows(e_refs, e_layout, ec, fw)
    fill_rows(x_refs, x_layout, xc, fw, dec)
    lat = lat_ref[...]
    back = nt_dot(ec[...], wc[...])
    slope = jnp.where(lat > 0, back, 0.0).astype(BF)
    bias = jnp.sum(slope.astype(F32), axis=0, keepdims=True).astype(BF)
    lat_t, slope_t = lat.T, slope.T
    for part, out in enumerate((own_out, sib_out)):
        out[SPAN:, :SPAN] = jnp.broadcast_to(bias[:, part * SPAN : (part + 1) * SPAN], (EXTRA, SPAN))
    for j in range(ns):
        cols = slice(j * fw, (j + 1) * fw)
        grad = jnp.dot(lat_t, ec[:, cols], preferred_element_type=F32) + jnp.dot(
            slope_t, xc[:, cols], preferred_element_type=F32
        )
        own_out[:SPAN, cols] = grad[:SPAN].astype(BF)
        sib_out[:SPAN, cols] = grad[SPAN:].astype(BF)


def sum_kernel(terms, meta, *refs):
    w_refs, b_refs = refs[:terms], refs[terms : 2 * terms]
    w_out, b_out = refs[2 * terms :]
    j, k = pl.program_id(0), pl.program_id(1)
    w_out[...] = jnp.zeros_like(w_out)
    for i in range(terms):

        @pl.when(meta[i] == k)
        def _(i=i):
            w_out[0] += w_refs[i][...].astype(F32)

    @pl.when((j == 0) & (k == 0))
    def _():
        b_out[...] = jnp.zeros_like(b_out)

    @pl.when(j == 0)
    def _():
        for i in range(terms):

            @pl.when(meta[i] == k)
            def _(i=i):
                b_out[pl.ds(k, 1)] += b_refs[i][0:1].astype(F32)[None]


def shards(activations, dictionary, enc_bias, dec_bias, block_codes):
    nd, npar = lax.axis_size("dict"), lax.axis_size("dp")
    nz = npar // 2
    s, d = lax.axis_index("dict"), lax.axis_index("dp")
    tokens, share = activations.shape
    width = dictionary.shape[1]
    own_blocks = dictionary.shape[0] // SPAN
    shard_blocks = own_blocks * npar
    ntb = block_codes.shape[0]
    aligned = share % SPAN == 0
    ns, fw = (nd, share) if aligned else (1, width)

    mine = lax.dynamic_index_in_dim(block_codes, s, axis=1, keepdims=False)
    codes = lax.all_gather(mine, "dp", axis=0, tiled=False)
    filled = codes >= 0
    local = codes - s * shard_blocks
    owner = jnp.where(filled, local // own_blocks, -1)
    inner = jnp.where(filled, local % own_blocks, -1)

    def pick(holder):
        match = owner == holder
        return jnp.max(jnp.where(match, inner, -1), axis=(1, 2)), jnp.any(match, axis=2).astype(jnp.int32)

    own_pick, own_named = pick(d)
    sib_pick, sib_named = pick(d ^ 1)

    order = s ^ jnp.arange(nd, dtype=jnp.int32)
    dec_rel = dec_bias.reshape(nd, share)[order].reshape(1, width)
    table = dictionary
    if not aligned:
        table = table.reshape(-1, nd, share)[:, order].reshape(-1, width)
    own_w = table.reshape(own_blocks, SPAN, width)
    sib_w = to_sibling(own_w)
    own_b = enc_bias.reshape(own_blocks, SPAN)
    sib_b = to_sibling(own_b)
    place = order if aligned else jnp.zeros((1,), jnp.int32)

    def meta_of(t):
        g = (d + 2 * (nz - t)) % npar
        safe = jnp.maximum(jnp.stack([own_pick[g], sib_pick[g]]), 0)
        named = jnp.stack([own_named[g], sib_named[g]], axis=1).reshape(-1)
        bias = jnp.concatenate([own_b[safe[0]], sib_b[safe[1]]]).astype(F32).reshape(1, 2 * SPAN)
        return jnp.concatenate([safe, named, place]), bias

    base = 2 + 2 * ntb

    def w_specs():
        return [
            pl.BlockSpec((1, SPAN, fw), lambda i, m, part=part, j=j: (m[part], 0, m[base + j]))
            for part in range(2)
            for j in range(ns)
        ]

    def whole(shape):
        return pl.BlockSpec(shape, lambda i, m: (0,) * len(shape))

    def flatten(slots):
        if not aligned:
            slots = [[jnp.concatenate(q, axis=0) if len(q) > 1 else q[0]] for q in slots]
            return [jnp.concatenate([q[0] for q in slots], axis=1)], [(0, 0, tokens)]
        pieces, layout = [], []
        for j, slot in enumerate(slots):
            row = 0
            for piece in slot:
                pieces.append(piece)
                layout.append((j, row, piece.shape[0]))
                row += piece.shape[0]
        return pieces, layout

    half = tokens // 2

    def forward(slots, meta, bias):
        pieces, layout = flatten(slots)
        if aligned:
            out_layout = [(j, h * half, half) for j in range(ns) for h in (0, 1)]
            dtypes = []
            for j in range(ns):
                for h in (0, 1):
                    fed = any(k & j == j and k.bit_count() == j.bit_count() + 1 and k ^ hop_bit(k, h) == j for k in range(1, nd))
                    dtypes.append(F32 if fed else BF)
        else:
            out_layout, dtypes = [(0, 0, tokens)], [F32]
        res = pl.pallas_call(
            functools.partial(fwd_kernel, layout, ns, fw, out_layout),
            grid_spec=pltpu.PrefetchScalarGridSpec(
                num_scalar_prefetch=1,
                grid=(1,),
                in_specs=[whole(p.shape) for p in pieces]
                + w_specs()
                + [whole((1, width)), whole((1, 2 * SPAN))],
                out_specs=[whole((tokens, 2 * SPAN))] + [whole((c, fw)) for _, _, c in out_layout],
                scratch_shapes=[pltpu.VMEM((tokens, width), BF), pltpu.VMEM((2 * SPAN, width), BF)],
            ),
            out_shape=[jax.ShapeDtypeStruct((tokens, 2 * SPAN), BF)]
            + [jax.ShapeDtypeStruct((c, fw), t) for (_, _, c), t in zip(out_layout, dtypes)],
            compiler_params=pltpu.CompilerParams(vmem_limit_bytes=VMEM_LIMIT),
            cost_estimate=pl.CostEstimate(
                flops=8 * tokens * SPAN * width, bytes_accessed=8 * tokens * width, transcendentals=0
            ),
        )(meta, *pieces, *([own_w] * ns), *([sib_w] * ns), dec_rel, bias)
        lat, outs = res[0], res[1:]
        if aligned:
            return lat, [[outs[2 * j], outs[2 * j + 1]] for j in range(nd)]
        full = outs[0].reshape(2, half, nd, share)
        return lat, [[full[h, :, j] for h in (0, 1)] for j in range(nd)]

    def backward(x_slots, e_slots, lat, meta):
        xp, xl = flatten(x_slots)
        ep, el = flatten(e_slots)
        rows = SPAN + EXTRA
        return pl.pallas_call(
            functools.partial(bwd_kernel, xl, el, ns, fw),
            grid_spec=pltpu.PrefetchScalarGridSpec(
                num_scalar_prefetch=1,
                grid=(1,),
                in_specs=[whole(p.shape) for p in xp + ep]
                + w_specs()
                + [whole((1, width)), whole((tokens, 2 * SPAN))],
                out_specs=[whole((rows, width))] * 2,
                scratch_shapes=[
                    pltpu.VMEM((tokens, width), BF),
                    pltpu.VMEM((tokens, width), BF),
                    pltpu.VMEM((2 * SPAN, width), BF),
                ],
            ),
            out_shape=[jax.ShapeDtypeStruct((rows, width), BF)] * 2,
            compiler_params=pltpu.CompilerParams(vmem_limit_bytes=VMEM_LIMIT),
            cost_estimate=pl.CostEstimate(
                flops=12 * tokens * SPAN * width, bytes_accessed=10 * tokens * width, transcendentals=0
            ),
        )(meta, *xp, *ep, *([own_w] * ns), *([sib_w] * ns), dec_rel, lat)

    metas = [meta_of(t) for t in range(nz)]
    own_x = [activations]
    for t in range(1, nz):
        own_x.append(along_ring(own_x[-1]))
    x_slots, lats, parts = [], [], []
    for t in range(nz):
        x_slots.append(gather_slots(own_x[t]))
        lat, part = forward(x_slots[t], *metas[t])
        lats.append(lat)
        parts.append(part)
    carry = None
    for t in list(range(1, nz)) + [0]:
        total = scatter_sum(parts[t])
        if carry is not None:
            total = total + along_ring(carry.astype(BF)).astype(F32)
        carry = total
    dec_own = lax.dynamic_slice_in_dim(dec_bias, s * share, share)
    error = (carry + dec_own - activations.astype(F32)).astype(BF)

    own_e = error
    own_terms, sib_terms = [], []
    for t in range(nz):
        if t:
            own_e = along_ring(own_e)
        mine_t, theirs = backward(x_slots[t], gather_slots(own_e), lats[t], metas[t][0])
        own_terms.append(mine_t)
        sib_terms.append(to_sibling(theirs))

    here = [(d + 2 * (nz - t)) % npar for t in range(nz)]
    which = jnp.stack([own_pick[g] for g in here] + [own_pick[g ^ 1] for g in here])
    terms = own_terms + sib_terms
    nt = len(terms)
    meta = jnp.concatenate([which, place])
    grad_w, grad_b = pl.pallas_call(
        functools.partial(sum_kernel, nt),
        grid_spec=pltpu.PrefetchScalarGridSpec(
            num_scalar_prefetch=1,
            grid=(ns, own_blocks),
            in_specs=[pl.BlockSpec((SPAN, fw), lambda j, k, m: (0, j))] * nt
            + [pl.BlockSpec((EXTRA, SPAN), lambda j, k, m: (SPAN // EXTRA, 0))] * nt,
            out_specs=[
                pl.BlockSpec((1, SPAN, fw), lambda j, k, m: (k, 0, m[nt + j])),
                pl.BlockSpec((own_blocks, 1, SPAN), lambda j, k, m: (0, 0, 0)),
            ],
        ),
        out_shape=[
            jax.ShapeDtypeStruct((own_blocks, SPAN, width), F32),
            jax.ShapeDtypeStruct((own_blocks, 1, SPAN), F32),
        ],
        compiler_params=pltpu.CompilerParams(vmem_limit_bytes=VMEM_LIMIT),
        cost_estimate=pl.CostEstimate(
            flops=nt * SPAN * width,
            bytes_accessed=2 * nt * SPAN * width + 4 * own_blocks * SPAN * width,
            transcendentals=0,
        ),
    )(meta, *terms, *terms)
    grad_w = grad_w.reshape(own_blocks * SPAN, width)
    if not aligned:
        grad_w = grad_w.reshape(-1, nd, share)[:, order].reshape(-1, width)
    return error, grad_w, grad_b.reshape(own_blocks * SPAN)


def solution(mesh):
    in_specs = (
        P("dp", "dict"),
        P(("dict", "dp"), None),
        P(("dict", "dp")),
        P(),
        P("dp", None, None),
    )
    out_specs = (P("dp", "dict"), P(("dict", "dp"), None), P(("dict", "dp")))
    return jax.shard_map(shards, mesh=mesh, in_specs=in_specs, out_specs=out_specs, check_vma=False)
```

```python
import functools

import jax
import jax.numpy as jnp
from jax import lax
from jax.experimental import pallas as pl
from jax.experimental.pallas import tpu as pltpu
from jax.sharding import PartitionSpec as P

SPAN = 128
EXTRA = 16
VMEM_LIMIT = 30 * 1024 * 1024
BF = jnp.bfloat16
F32 = jnp.float32


def hop_bit(slot, half):
    return 1 << (slot.bit_length() - 1) if half == 0 else slot & -slot


class Steps:
    def __init__(self):
        self.done = []

    def send(self, items, after=()):
        held = list(after) + (self.done[-2] if len(self.done) > 1 else [])
        out = []
        for x, bit in items:
            if held:
                x = lax.optimization_barrier((x, *held))[0]
            out.append(over_dict(x, bit))
        self.done.append(out)
        return out


def over_dict(x, bit):
    n = lax.axis_size("dict")
    return lax.ppermute(x, "dict", [(i, i ^ bit) for i in range(n)])


def to_sibling(x):
    n = lax.axis_size("dp")
    return lax.ppermute(x, "dp", [(i, i ^ 1) for i in range(n)])


def along_ring(x):
    n = lax.axis_size("dp")
    return lax.ppermute(x, "dp", [(i, (i + 2) % n) for i in range(n)])


def gather_level(slots, count, mode):
    n = lax.axis_size("dict")
    items, keys = [], []
    for slot in range(1, n):
        if slot.bit_count() != count:
            continue
        if count == 1 or mode < 2:
            bit = hop_bit(slot, mode % 2)
            source = slots[slot ^ bit]
            items.append((source[0] if len(source) == 1 else jnp.concatenate(source, axis=0), bit))
            keys.append((slot, 0))
        else:
            for h in (0, 1):
                bit = hop_bit(slot, h)
                source = slots[slot ^ bit]
                if len(source) == 1:
                    half = source[0].shape[0] // 2
                    items.append((source[0][h * half : (h + 1) * half], bit))
                else:
                    items.append((source[h], bit))
                keys.append((slot, h))
    return items, keys


def gather_store(slots, keys, got):
    for (slot, _), x in zip(keys, got):
        slots.setdefault(slot, []).append(x)


def scatter_level(acc, count):
    n = lax.axis_size("dict")
    items, keys = [], []
    for slot in range(1, n):
        if slot.bit_count() != count:
            continue
        if len(acc[slot]) == 1:
            bit = slot
            items.append((acc[slot][0].astype(BF), bit))
            keys.append((0, None))
        else:
            for h in (0, 1):
                bit = hop_bit(slot, h)
                items.append((acc[slot][h].astype(BF), bit))
                keys.append((slot ^ bit, h))
    return items, keys


def scatter_store(acc, keys, got):
    for (slot, h), x in zip(keys, got):
        x = x.astype(F32)
        if h is None:
            acc[slot] = [acc[slot][0] + x]
        elif len(acc[slot]) == 2:
            acc[slot][h] = acc[slot][h] + x
        else:
            half = x.shape[0]
            grow = ((0, half), (0, 0)) if h == 0 else ((half, 0), (0, 0))
            acc[slot] = [acc[slot][0] + jnp.pad(x, grow)]


def nt_dot(a, b):
    return lax.dot_general(a, b, (((1,), (1,)), ((), ())), preferred_element_type=F32)


def fill_weights(w_refs, w_cat, fw):
    ns = len(w_refs) // 2
    for part in range(2):
        for j in range(ns):
            w_cat[part * SPAN : (part + 1) * SPAN, j * fw : (j + 1) * fw] = w_refs[part * ns + j][0]


def fill_rows(refs, layout, dst, fw, dec=None):
    for ref, (slot, row, count) in zip(refs, layout):
        cols = slice(slot * fw, (slot + 1) * fw)
        value = ref[...]
        if dec is not None:
            value = (value.astype(F32) - dec[:, cols]).astype(BF)
        dst[row : row + count, cols] = value


def fwd_kernel(layout, ns, fw, out_layout, meta, *refs):
    nx = len(layout)
    x_refs, refs = refs[:nx], refs[nx:]
    w_refs, refs = refs[: 2 * ns], refs[2 * ns :]
    dec, own_bias, sib_bias, lat_out = refs[:4]
    outs = refs[4 : 4 + len(out_layout)]
    xc, wc = refs[4 + len(out_layout) :]
    fill_weights(w_refs, wc, fw)
    fill_rows(x_refs, layout, xc, fw, dec)
    preact = nt_dot(xc[...], wc[...])
    biases = (own_bias[0].astype(F32), sib_bias[0].astype(F32))
    tokens = preact.shape[0]
    for tb in range(tokens // SPAN):
        for part in range(2):
            cell = (slice(tb * SPAN, (tb + 1) * SPAN), slice(part * SPAN, (part + 1) * SPAN))
            named = jnp.full((SPAN, SPAN), meta[2 + 2 * tb + part], jnp.int32) > 0
            lat_out[cell] = jnp.where(named, jnp.maximum(preact[cell] + biases[part], 0.0), 0.0).astype(BF)
    lat = lat_out[...]
    for j in range(ns):
        recon = jnp.dot(lat, wc[:, j * fw : (j + 1) * fw], preferred_element_type=F32)
        for out, (slot, row, count) in zip(outs, out_layout):
            if slot == j:
                out[...] = recon[row : row + count].astype(out.dtype)


def bwd_kernel(x_layout, e_layout, ns, fw, meta, *refs):
    nx, ne = len(x_layout), len(e_layout)
    x_refs, refs = refs[:nx], refs[nx:]
    e_refs, refs = refs[:ne], refs[ne:]
    w_refs, refs = refs[: 2 * ns], refs[2 * ns :]
    dec, lat_ref, own_out, sib_out, xc, ec, wc = refs
    fill_weights(w_refs, wc, fw)
    fill_rows(e_refs, e_layout, ec, fw)
    fill_rows(x_refs, x_layout, xc, fw, dec)
    lat = lat_ref[...]
    back = nt_dot(ec[...], wc[...])
    slope = jnp.where(lat > 0, back, 0.0).astype(BF)
    bias = jnp.sum(slope.astype(F32), axis=0, keepdims=True).astype(BF)
    lat_t, slope_t = lat.T, slope.T
    for part, out in enumerate((own_out, sib_out)):
        out[SPAN:, :SPAN] = jnp.broadcast_to(bias[:, part * SPAN : (part + 1) * SPAN], (EXTRA, SPAN))
    for j in range(ns):
        cols = slice(j * fw, (j + 1) * fw)
        grad = jnp.dot(lat_t, ec[:, cols], preferred_element_type=F32) + jnp.dot(
            slope_t, xc[:, cols], preferred_element_type=F32
        )
        own_out[:SPAN, cols] = grad[:SPAN].astype(BF)
        sib_out[:SPAN, cols] = grad[SPAN:].astype(BF)


def sum_kernel(terms, meta, *refs):
    w_refs, b_refs = refs[:terms], refs[terms : 2 * terms]
    w_out, b_out = refs[2 * terms :]
    w_out[...] = jnp.zeros_like(w_out)
    for i in range(terms):
        block = meta[i]

        @pl.when(block >= 0)
        def _(i=i, block=block):
            w_out[block] += w_refs[i][...].astype(F32)

    @pl.when((pl.program_id(0) == 0) & (pl.program_id(1) == 0))
    def _():
        b_out[...] = jnp.zeros_like(b_out)
        for i in range(terms):
            block = meta[i]

            @pl.when(block >= 0)
            def _(i=i, block=block):
                b_out[block] += b_refs[i][0:1].astype(F32)


def shards(activations, dictionary, enc_bias, dec_bias, block_codes):
    nd, npar = lax.axis_size("dict"), lax.axis_size("dp")
    nz = npar // 2
    s, d = lax.axis_index("dict"), lax.axis_index("dp")
    tokens, share = activations.shape
    width = dictionary.shape[1]
    own_blocks = dictionary.shape[0] // SPAN
    shard_blocks = own_blocks * npar
    ntb = block_codes.shape[0]
    aligned = share % SPAN == 0
    ns, fw = (nd, share) if aligned else (1, width)

    ring_x = [activations]
    for t in range(1, nz):
        ring_x.append(along_ring(ring_x[-1]))
    codes = [lax.dynamic_index_in_dim(block_codes, s, axis=1, keepdims=False)]
    for t in range(1, nz):
        codes.append(along_ring(codes[-1]))
    codes = jnp.stack(codes)
    codes = jnp.concatenate([codes, to_sibling(codes)])
    filled = codes >= 0
    local = codes - s * shard_blocks
    owner = jnp.where(filled, local // own_blocks, -1)
    inner = jnp.where(filled, local % own_blocks, -1)
    holders = jnp.stack([d, d ^ 1])[:, None, None, None]
    match = owner == holders
    picked = jnp.max(jnp.where(match, inner, -1), axis=(2, 3))
    named = jnp.any(match, axis=3).astype(jnp.int32)

    order = s ^ jnp.arange(nd, dtype=jnp.int32)
    dec_rel = dec_bias.reshape(nd, share)[order].reshape(1, width)
    table = dictionary
    if not aligned:
        table = table.reshape(-1, nd, share)[:, order].reshape(-1, width)
    own_w = table.reshape(own_blocks, SPAN, width)
    sib_w = to_sibling(own_w)
    own_b = enc_bias.reshape(own_blocks, 1, SPAN)
    sib_b = to_sibling(own_b)
    place = order if aligned else jnp.zeros((1,), jnp.int32)

    metas = jnp.concatenate(
        [
            jnp.maximum(picked[:, :nz], 0).T,
            named[:, :nz].transpose(1, 2, 0).reshape(nz, 2 * ntb),
            jnp.broadcast_to(place, (nz, place.shape[0])),
        ],
        axis=1,
    )
    metas = [metas[t] for t in range(nz)]
    base = 2 + 2 * ntb

    def w_specs():
        return [
            pl.BlockSpec((1, SPAN, fw), lambda i, m, part=part, j=j: (m[part], 0, m[base + j]))
            for part in range(2)
            for j in range(ns)
        ]

    def b_specs():
        return [
            pl.BlockSpec((1, 1, SPAN), lambda i, m, part=part: (m[part], 0, 0)) for part in range(2)
        ]

    def whole(shape):
        return pl.BlockSpec(shape, lambda i, m: (0,) * len(shape))

    def flatten(slots):
        if not aligned:
            slots = [[jnp.concatenate(q, axis=0) if len(q) > 1 else q[0]] for q in slots]
            return [jnp.concatenate([q[0] for q in slots], axis=1)], [(0, 0, tokens)]
        pieces, layout = [], []
        for j, slot in enumerate(slots):
            row = 0
            for piece in slot:
                pieces.append(piece)
                layout.append((j, row, piece.shape[0]))
                row += piece.shape[0]
        return pieces, layout

    half = tokens // 2

    def forward(slots, meta):
        pieces, layout = flatten(slots)
        if aligned:
            out_layout, dtypes = [], []
            for j in range(nd):
                if j.bit_count() < 2:
                    out_layout.append((j, 0, tokens))
                    dtypes.append(F32)
                else:
                    out_layout += [(j, 0, half), (j, half, half)]
                    dtypes += [BF if j == nd - 1 else F32] * 2
        else:
            out_layout, dtypes = [(0, 0, tokens)], [F32]
        res = pl.pallas_call(
            functools.partial(fwd_kernel, layout, ns, fw, out_layout),
            grid_spec=pltpu.PrefetchScalarGridSpec(
                num_scalar_prefetch=1,
                grid=(1,),
                in_specs=[whole(p.shape) for p in pieces]
                + w_specs()
                + [whole((1, width))]
                + b_specs(),
                out_specs=[whole((tokens, 2 * SPAN))] + [whole((c, fw)) for _, _, c in out_layout],
                scratch_shapes=[pltpu.VMEM((tokens, width), BF), pltpu.VMEM((2 * SPAN, width), BF)],
            ),
            out_shape=[jax.ShapeDtypeStruct((tokens, 2 * SPAN), BF)]
            + [jax.ShapeDtypeStruct((c, fw), t) for (_, _, c), t in zip(out_layout, dtypes)],
            compiler_params=pltpu.CompilerParams(vmem_limit_bytes=VMEM_LIMIT),
            cost_estimate=pl.CostEstimate(
                flops=8 * tokens * SPAN * width, bytes_accessed=8 * tokens * width, transcendentals=0
            ),
        )(meta, *pieces, *([own_w] * ns), *([sib_w] * ns), dec_rel, own_b, sib_b)
        lat, outs = res[0], res[1:]
        if aligned:
            acc = {}
            for out, (j, _, _) in zip(outs, out_layout):
                acc.setdefault(j, []).append(out)
            return lat, acc
        full = outs[0].reshape(tokens, nd, share)
        split = {j: [full[:, j]] if j.bit_count() < 2 else [full[:half, j], full[half:, j]] for j in range(nd)}
        return lat, split

    def backward(x_slots, e_slots, lat, meta):
        xp, xl = flatten(x_slots)
        ep, el = flatten(e_slots)
        rows = SPAN + EXTRA
        return pl.pallas_call(
            functools.partial(bwd_kernel, xl, el, ns, fw),
            grid_spec=pltpu.PrefetchScalarGridSpec(
                num_scalar_prefetch=1,
                grid=(1,),
                in_specs=[whole(p.shape) for p in xp + ep]
                + w_specs()
                + [whole((1, width)), whole((tokens, 2 * SPAN))],
                out_specs=[whole((rows, width))] * 2,
                scratch_shapes=[
                    pltpu.VMEM((tokens, width), BF),
                    pltpu.VMEM((tokens, width), BF),
                    pltpu.VMEM((2 * SPAN, width), BF),
                ],
            ),
            out_shape=[jax.ShapeDtypeStruct((rows, width), BF)] * 2,
            compiler_params=pltpu.CompilerParams(vmem_limit_bytes=VMEM_LIMIT),
            cost_estimate=pl.CostEstimate(
                flops=12 * tokens * SPAN * width, bytes_accessed=10 * tokens * width, transcendentals=0
            ),
        )(meta, *xp, *ep, *([own_w] * ns), *([sib_w] * ns), dec_rel, lat)

    levels = nd.bit_length() - 1
    paired = nd == 4 and nz == 4
    steps = Steps()
    x_slots = [{0: [x]} for x in ring_x]
    x_left = {}

    def x_step(*jobs):
        items, spans = [], []
        for t, count, mode in jobs:
            more, keys = gather_level(x_slots[t], count, mode)
            spans.append((t, keys, len(items)))
            items += more
        got = steps.send(items)
        for t, keys, at in spans:
            gather_store(x_slots[t], keys, got[at : at + len(keys)])

    lats, accs = {}, {}

    def encode(t):
        lats[t], accs[t] = forward([x_slots[t][j] for j in range(nd)], metas[t])

    def r_step(t, count):
        items, keys = scatter_level(accs[t], count)
        scatter_store(accs[t], keys, steps.send(items))

    if paired:
        x_step((0, 1, 0))
        x_step((1, 1, 0))
        x_step((0, 2, 0), (1, 2, 1))
        encode(1)
        encode(0)
        x_step((2, 1, 0))
        r_step(1, 2)
        x_step((3, 1, 0))
        x_step((2, 2, 0), (3, 2, 1))
        r_step(1, 1)
        encode(2)
        r_step(2, 2)
        encode(3)
        r_step(3, 2)
        r_step(2, 1)
        r_step(0, 2)
        r_step(3, 1)
        r_step(0, 1)
    else:
        for t in range(nz):
            for count in range(1, levels + 1):
                x_step((t, count, 2))
            encode(t)
        for t in list(range(1, nz)) + [0]:
            for count in range(levels, 0, -1):
                r_step(t, count)
    carry = None
    for t in list(range(1, nz)) + [0]:
        total = accs[t][0][0]
        if carry is not None:
            total = total + along_ring(carry.astype(BF)).astype(F32)
        carry = total
    dec_own = lax.dynamic_slice_in_dim(dec_bias, s * share, share)
    error = (carry + dec_own - activations.astype(F32)).astype(BF)

    ring_e = [error]
    for t in range(1, nz):
        ring_e.append(along_ring(ring_e[-1]))
    e_slots = [{0: [e]} for e in ring_e]
    own_terms, sib_terms = {}, {}
    steps = Steps()

    def e_step(*jobs, after=()):
        items, spans = [], []
        for t, count, mode in jobs:
            more, keys = gather_level(e_slots[t], count, mode)
            spans.append((t, keys, len(items)))
            items += more
        got = steps.send(items, after)
        for t, keys, at in spans:
            gather_store(e_slots[t], keys, got[at : at + len(keys)])

    def decode(t):
        own_terms[t], theirs = backward(
            [x_slots[t][j] for j in range(nd)], [e_slots[t][j] for j in range(nd)], lats[t], metas[t]
        )
        sib_terms[t] = to_sibling(theirs)

    if paired:
        e_step((0, 1, 0))
        e_step((1, 1, 0))
        e_step((0, 2, 0), (1, 2, 1))
        e_step((2, 1, 0))
        decode(0)
        decode(1)
        e_step((2, 2, 2))
        e_step((3, 1, 0), after=[own_terms[0]])
        e_step((3, 2, 2), after=[own_terms[1]])
        decode(2)
        decode(3)
    else:
        for t in range(nz):
            for count in range(1, levels + 1):
                e_step((t, count, 2))
            decode(t)
    own_terms = [own_terms[t] for t in range(nz)]
    sib_terms = [sib_terms[t] for t in range(nz)]

    which = picked[0]
    terms = own_terms + sib_terms
    nt = len(terms)
    meta = jnp.concatenate([which, place])
    grad_w, grad_b = pl.pallas_call(
        functools.partial(sum_kernel, nt),
        grid_spec=pltpu.PrefetchScalarGridSpec(
            num_scalar_prefetch=1,
            grid=(ns, 2),
            in_specs=[pl.BlockSpec((SPAN // 2, fw), lambda j, k, m: (k, j))] * nt
            + [pl.BlockSpec((EXTRA, SPAN), lambda j, k, m: (SPAN // EXTRA, 0))] * nt,
            out_specs=[
                pl.BlockSpec((own_blocks, SPAN // 2, fw), lambda j, k, m: (0, k, m[nt + j])),
                pl.BlockSpec((own_blocks, 1, SPAN), lambda j, k, m: (0, 0, 0)),
            ],
        ),
        out_shape=[
            jax.ShapeDtypeStruct((own_blocks, SPAN, width), F32),
            jax.ShapeDtypeStruct((own_blocks, 1, SPAN), F32),
        ],
        compiler_params=pltpu.CompilerParams(vmem_limit_bytes=VMEM_LIMIT),
        cost_estimate=pl.CostEstimate(
            flops=nt * SPAN * width,
            bytes_accessed=2 * nt * SPAN * width + 4 * own_blocks * SPAN * width,
            transcendentals=0,
        ),
    )(meta, *terms, *terms)
    grad_w = grad_w.reshape(own_blocks * SPAN, width)
    if not aligned:
        grad_w = grad_w.reshape(-1, nd, share)[:, order].reshape(-1, width)
    return error, grad_w, grad_b.reshape(own_blocks * SPAN)


def solution(mesh):
    in_specs = (
        P("dp", "dict"),
        P(("dict", "dp"), None),
        P(("dict", "dp")),
        P(),
        P("dp", None, None),
    )
    out_specs = (P("dp", "dict"), P(("dict", "dp"), None), P(("dict", "dp")))
    return jax.shard_map(shards, mesh=mesh, in_specs=in_specs, out_specs=out_specs, check_vma=False)
```

```python
import functools

import jax
import jax.numpy as jnp
from jax import lax
from jax.experimental import pallas as pl
from jax.experimental.pallas import tpu as pltpu
from jax.sharding import PartitionSpec as P

SPAN = 128
EXTRA = 16
VMEM_LIMIT = 30 * 1024 * 1024
PLAN_X = (
    "a010", "a110 S0", "a020 a121", "k1", "k0", "a210", "r12", "a310", "a220 a321", "r11",
    "k2", "r22", "k3", "r32", "r21", "r31", "r02", "r01",
)
PLAN_E = (
    "a010", "a110", "a020 a121", "a210", "d0", "d1", "a222", "a310 D0", "a322 D1", "d2", "d3",
)
DEPTH = 2
BF = jnp.bfloat16
F32 = jnp.float32


def hop_bit(slot, half):
    return 1 << (slot.bit_length() - 1) if half == 0 else slot & -slot


class Steps:
    def __init__(self):
        self.done = []

    def send(self, items, after=(), depth=DEPTH):
        held = list(after) + (self.done[-depth] if len(self.done) >= depth > 0 else [])
        out = []
        for x, bit in items:
            if held:
                x = lax.optimization_barrier((x, *held))[0]
            out.append(over_dict(x, bit))
        self.done.append(out)
        return out


def over_dict(x, bit):
    n = lax.axis_size("dict")
    return lax.ppermute(x, "dict", [(i, i ^ bit) for i in range(n)])


def to_sibling(x):
    n = lax.axis_size("dp")
    return lax.ppermute(x, "dp", [(i, i ^ 1) for i in range(n)])


def along_ring(x):
    n = lax.axis_size("dp")
    return lax.ppermute(x, "dp", [(i, (i + 2) % n) for i in range(n)])


def gather_level(slots, count, mode):
    n = lax.axis_size("dict")
    items, keys = [], []
    for slot in range(1, n):
        if slot.bit_count() != count:
            continue
        if count == 1 or mode < 2:
            bit = hop_bit(slot, mode % 2)
            source = slots[slot ^ bit]
            items.append((source[0] if len(source) == 1 else jnp.concatenate(source, axis=0), bit))
            keys.append((slot, 0))
        else:
            for h in (0, 1):
                bit = hop_bit(slot, h)
                source = slots[slot ^ bit]
                if len(source) == 1:
                    half = source[0].shape[0] // 2
                    items.append((source[0][h * half : (h + 1) * half], bit))
                else:
                    items.append((source[h], bit))
                keys.append((slot, h))
    return items, keys


def gather_store(slots, keys, got):
    for (slot, _), x in zip(keys, got):
        slots.setdefault(slot, []).append(x)


def scatter_level(acc, count):
    n = lax.axis_size("dict")
    items, keys = [], []
    for slot in range(1, n):
        if slot.bit_count() != count:
            continue
        if len(acc[slot]) == 1:
            bit = slot
            items.append((acc[slot][0].astype(BF), bit))
            keys.append((0, None))
        else:
            for h in (0, 1):
                bit = hop_bit(slot, h)
                items.append((acc[slot][h].astype(BF), bit))
                keys.append((slot ^ bit, h))
    return items, keys


def scatter_store(acc, keys, got):
    for (slot, h), x in zip(keys, got):
        x = x.astype(F32)
        if h is None:
            acc[slot] = [acc[slot][0] + x]
        elif len(acc[slot]) == 2:
            acc[slot][h] = acc[slot][h] + x
        else:
            half = x.shape[0]
            grow = ((0, half), (0, 0)) if h == 0 else ((half, 0), (0, 0))
            acc[slot] = [acc[slot][0] + jnp.pad(x, grow)]


def nt_dot(a, b):
    return lax.dot_general(a, b, (((1,), (1,)), ((), ())), preferred_element_type=F32)


def fill_weights(w_refs, w_cat, fw):
    ns = len(w_refs) // 2
    for part in range(2):
        for j in range(ns):
            w_cat[part * SPAN : (part + 1) * SPAN, j * fw : (j + 1) * fw] = w_refs[part * ns + j][0]


def fill_rows(refs, layout, dst, fw, dec=None):
    for ref, (slot, row, count) in zip(refs, layout):
        cols = slice(slot * fw, (slot + 1) * fw)
        value = ref[...]
        if dec is not None:
            value = (value.astype(F32) - dec[:, cols]).astype(BF)
        dst[row : row + count, cols] = value


def fwd_kernel(layout, ns, fw, out_layout, meta, *refs):
    nx = len(layout)
    x_refs, refs = refs[:nx], refs[nx:]
    w_refs, refs = refs[: 2 * ns], refs[2 * ns :]
    dec, own_bias, sib_bias, lat_out = refs[:4]
    outs = refs[4 : 4 + len(out_layout)]
    xc, wc = refs[4 + len(out_layout) :]
    fill_weights(w_refs, wc, fw)
    fill_rows(x_refs, layout, xc, fw, dec)
    preact = nt_dot(xc[...], wc[...])
    biases = (own_bias[0].astype(F32), sib_bias[0].astype(F32))
    tokens = preact.shape[0]
    for tb in range(tokens // SPAN):
        for part in range(2):
            cell = (slice(tb * SPAN, (tb + 1) * SPAN), slice(part * SPAN, (part + 1) * SPAN))
            named = jnp.full((SPAN, SPAN), meta[2 + 2 * tb + part], jnp.int32) > 0
            lat_out[cell] = jnp.where(named, jnp.maximum(preact[cell] + biases[part], 0.0), 0.0).astype(BF)
    lat = lat_out[...]
    for j in range(ns):
        recon = jnp.dot(lat, wc[:, j * fw : (j + 1) * fw], preferred_element_type=F32)
        for out, (slot, row, count) in zip(outs, out_layout):
            if slot == j:
                out[...] = recon[row : row + count].astype(out.dtype)


def bwd_kernel(x_layout, e_layout, ns, fw, meta, *refs):
    nx, ne = len(x_layout), len(e_layout)
    x_refs, refs = refs[:nx], refs[nx:]
    e_refs, refs = refs[:ne], refs[ne:]
    w_refs, refs = refs[: 2 * ns], refs[2 * ns :]
    dec, lat_ref, own_out, sib_out, xc, ec, wc = refs
    fill_weights(w_refs, wc, fw)
    fill_rows(e_refs, e_layout, ec, fw)
    fill_rows(x_refs, x_layout, xc, fw, dec)
    lat = lat_ref[...]
    back = nt_dot(ec[...], wc[...])
    slope = jnp.where(lat > 0, back, 0.0).astype(BF)
    bias = jnp.sum(slope.astype(F32), axis=0, keepdims=True).astype(BF)
    lat_t, slope_t = lat.T, slope.T
    for part, out in enumerate((own_out, sib_out)):
        out[SPAN:, :SPAN] = jnp.broadcast_to(bias[:, part * SPAN : (part + 1) * SPAN], (EXTRA, SPAN))
    for j in range(ns):
        cols = slice(j * fw, (j + 1) * fw)
        grad = jnp.dot(lat_t, ec[:, cols], preferred_element_type=F32) + jnp.dot(
            slope_t, xc[:, cols], preferred_element_type=F32
        )
        own_out[:SPAN, cols] = grad[:SPAN].astype(BF)
        sib_out[:SPAN, cols] = grad[SPAN:].astype(BF)


def sum_kernel(terms, meta, *refs):
    w_refs, b_refs = refs[:terms], refs[terms : 2 * terms]
    w_out, b_out = refs[2 * terms :]
    w_out[...] = jnp.zeros_like(w_out)
    for i in range(terms):
        block = meta[i]

        @pl.when(block >= 0)
        def _(i=i, block=block):
            w_out[block] += w_refs[i][...].astype(F32)

    @pl.when((pl.program_id(0) == 0) & (pl.program_id(1) == 0))
    def _():
        b_out[...] = jnp.zeros_like(b_out)
        for i in range(terms):
            block = meta[i]

            @pl.when(block >= 0)
            def _(i=i, block=block):
                b_out[block] += b_refs[i][0:1].astype(F32)


def shards(activations, dictionary, enc_bias, dec_bias, block_codes):
    nd, npar = lax.axis_size("dict"), lax.axis_size("dp")
    nz = npar // 2
    s, d = lax.axis_index("dict"), lax.axis_index("dp")
    tokens, share = activations.shape
    width = dictionary.shape[1]
    own_blocks = dictionary.shape[0] // SPAN
    shard_blocks = own_blocks * npar
    ntb = block_codes.shape[0]
    aligned = share % SPAN == 0
    ns, fw = (nd, share) if aligned else (1, width)

    mine = lax.dynamic_index_in_dim(block_codes, s, axis=1, keepdims=False)
    everyone = lax.all_to_all(jnp.broadcast_to(mine, (npar, *mine.shape)), "dp", 0, 0)
    codes = [everyone[(d + 2 * (nz - t)) % npar] for t in range(nz)]
    ring_x = [activations]
    for t in range(1, nz):
        ring_x.append(along_ring(ring_x[-1]))

    def pick(codes):
        filled = codes >= 0
        local = codes - s * shard_blocks
        owner = jnp.where(filled, local // own_blocks, -1)
        inner = jnp.where(filled, local % own_blocks, -1)
        match = owner == jnp.stack([d, d ^ 1])[:, None, None, None]
        picked = jnp.max(jnp.where(match, inner, -1), axis=(2, 3))
        return picked, jnp.any(match, axis=3).astype(jnp.int32)

    order = s ^ jnp.arange(nd, dtype=jnp.int32)
    dec_rel = dec_bias.reshape(nd, share)[order].reshape(1, width)
    table = dictionary
    if not aligned:
        table = table.reshape(-1, nd, share)[:, order].reshape(-1, width)
    own_w = table.reshape(own_blocks, SPAN, width)
    sib_w = to_sibling(own_w)
    own_b = enc_bias.reshape(own_blocks, 1, SPAN)
    sib_b = to_sibling(own_b)
    place = order if aligned else jnp.zeros((1,), jnp.int32)

    def metas_of(codes):
        picked, named = pick(jnp.stack(codes))
        n = len(codes)
        metas = jnp.concatenate(
            [
                jnp.maximum(picked, 0).T,
                named.transpose(1, 2, 0).reshape(n, 2 * ntb),
                jnp.broadcast_to(place, (n, place.shape[0])),
            ],
            axis=1,
        )
        return [metas[t] for t in range(n)]

    metas = metas_of(codes)
    base = 2 + 2 * ntb

    def w_specs():
        return [
            pl.BlockSpec((1, SPAN, fw), lambda i, m, part=part, j=j: (m[part], 0, m[base + j]))
            for part in range(2)
            for j in range(ns)
        ]

    def b_specs():
        return [
            pl.BlockSpec((1, 1, SPAN), lambda i, m, part=part: (m[part], 0, 0)) for part in range(2)
        ]

    def whole(shape):
        return pl.BlockSpec(shape, lambda i, m: (0,) * len(shape))

    def flatten(slots):
        if not aligned:
            slots = [[jnp.concatenate(q, axis=0) if len(q) > 1 else q[0]] for q in slots]
            return [jnp.concatenate([q[0] for q in slots], axis=1)], [(0, 0, tokens)]
        pieces, layout = [], []
        for j, slot in enumerate(slots):
            row = 0
            for piece in slot:
                pieces.append(piece)
                layout.append((j, row, piece.shape[0]))
                row += piece.shape[0]
        return pieces, layout

    half = tokens // 2

    def forward(slots, meta, last):
        pieces, layout = flatten(slots)
        if aligned:
            out_layout, dtypes = [], []
            for j in range(nd):
                if j.bit_count() < 2:
                    out_layout.append((j, 0, tokens))
                    dtypes.append(F32)
                else:
                    out_layout += [(j, 0, half), (j, half, half)]
                    dtypes += [last if j == nd - 1 else F32] * 2
        else:
            out_layout, dtypes = [(0, 0, tokens)], [F32]
        res = pl.pallas_call(
            functools.partial(fwd_kernel, layout, ns, fw, out_layout),
            grid_spec=pltpu.PrefetchScalarGridSpec(
                num_scalar_prefetch=1,
                grid=(1,),
                in_specs=[whole(p.shape) for p in pieces]
                + w_specs()
                + [whole((1, width))]
                + b_specs(),
                out_specs=[whole((tokens, 2 * SPAN))] + [whole((c, fw)) for _, _, c in out_layout],
                scratch_shapes=[pltpu.VMEM((tokens, width), BF), pltpu.VMEM((2 * SPAN, width), BF)],
            ),
            out_shape=[jax.ShapeDtypeStruct((tokens, 2 * SPAN), BF)]
            + [jax.ShapeDtypeStruct((c, fw), t) for (_, _, c), t in zip(out_layout, dtypes)],
            compiler_params=pltpu.CompilerParams(vmem_limit_bytes=VMEM_LIMIT),
            cost_estimate=pl.CostEstimate(
                flops=8 * tokens * SPAN * width, bytes_accessed=8 * tokens * width, transcendentals=0
            ),
        )(meta, *pieces, *([own_w] * ns), *([sib_w] * ns), dec_rel, own_b, sib_b)
        lat, outs = res[0], res[1:]
        if aligned:
            acc = {}
            for out, (j, _, _) in zip(outs, out_layout):
                acc.setdefault(j, []).append(out)
            return lat, acc
        full = outs[0].reshape(tokens, nd, share)
        split = {j: [full[:, j]] if j.bit_count() < 2 else [full[:half, j], full[half:, j]] for j in range(nd)}
        return lat, split

    def backward(x_slots, e_slots, lat, meta):
        xp, xl = flatten(x_slots)
        ep, el = flatten(e_slots)
        rows = SPAN + EXTRA
        return pl.pallas_call(
            functools.partial(bwd_kernel, xl, el, ns, fw),
            grid_spec=pltpu.PrefetchScalarGridSpec(
                num_scalar_prefetch=1,
                grid=(1,),
                in_specs=[whole(p.shape) for p in xp + ep]
                + w_specs()
                + [whole((1, width)), whole((tokens, 2 * SPAN))],
                out_specs=[whole((rows, width))] * 2,
                scratch_shapes=[
                    pltpu.VMEM((tokens, width), BF),
                    pltpu.VMEM((tokens, width), BF),
                    pltpu.VMEM((2 * SPAN, width), BF),
                ],
            ),
            out_shape=[jax.ShapeDtypeStruct((rows, width), BF)] * 2,
            compiler_params=pltpu.CompilerParams(vmem_limit_bytes=VMEM_LIMIT),
            cost_estimate=pl.CostEstimate(
                flops=12 * tokens * SPAN * width, bytes_accessed=10 * tokens * width, transcendentals=0
            ),
        )(meta, *xp, *ep, *([own_w] * ns), *([sib_w] * ns), dec_rel, lat)

    levels = nd.bit_length() - 1
    paired = nd == 4 and nz == 4
    results = {"K": {}, "D": {}, "C": {t: c for t, c in enumerate(codes)}}
    accs, sib_terms = {}, {}

    def run(plan, slots):
        steps = Steps()
        fed = {int(w[1]) for line in plan for w in line.split() if w[0] == "h"}
        for line in plan:
            words = line.split()
            after, depth = [], DEPTH if paired else 0
            for w in words:
                if w[0] == "S":
                    after += steps.done[int(w[1:])]
                elif w[0] in results:
                    after.append(results[w[0]][int(w[1:])])
                elif w[0] == "/":
                    depth = int(w[1:])
            hold = lambda x: lax.optimization_barrier((x, *after))[0] if after else x
            items, stores = [], []
            for w in words:
                if w[0] not in "arkdgh":
                    continue
                t = int(w[1])
                if w[0] == "a":
                    more, keys = gather_level(slots[t], int(w[2]), int(w[3]))
                    stores.append((gather_store, slots[t], keys, len(items)))
                    items += more
                elif w[0] == "r":
                    more, keys = scatter_level(accs[t], int(w[2]))
                    stores.append((scatter_store, accs[t], keys, len(items)))
                    items += more
                elif w[0] == "k":
                    last = F32 if t - 1 in fed else BF
                    lat, accs[t] = forward([slots[t][j] for j in range(nd)], hold(metas[t]), last)
                    results["K"][t] = lat
                elif w[0] == "d":
                    results["D"][t], theirs = backward(
                        [x_slots[t][j] for j in range(nd)],
                        [slots[t][j] for j in range(nd)],
                        results["K"][t],
                        hold(metas[t]),
                    )
                    sib_terms[t] = to_sibling(theirs)
                elif w[0] == "g":
                    slots[t][nd - 1] = [along_ring(hold(x)) for x in slots[t - 1][nd - 1]]
                elif w[0] == "h":
                    moved = [along_ring(hold(x.astype(BF))) for x in accs[t].pop(nd - 1)]
                    accs[t + 1][nd - 1] = [x + y.astype(F32) for x, y in zip(accs[t + 1][nd - 1], moved)]
            if items:
                got = steps.send(items, after, depth)
                for store, where, keys, at in stores:
                    store(where, keys, got[at : at + len(keys)])

    ring_order = list(range(1, nz)) + [0]
    plan_x, plan_e = PLAN_X, PLAN_E
    if not paired:
        plan_x, plan_e = [], []
        for t in range(nz):
            gather = [f"a{t}{c}2" for c in range(1, levels + 1)]
            plan_x += gather + [f"k{t}"]
            plan_e += gather + [f"d{t}"]
        plan_x += [f"r{t}{c}" for t in ring_order for c in range(levels, 0, -1)]
    x_slots = [{0: [x]} for x in ring_x]
    run(plan_x, x_slots)
    carry = None
    for t in ring_order:
        total = accs[t][0][0]
        if carry is not None:
            total = total + along_ring(carry.astype(BF)).astype(F32)
        carry = total
    dec_own = lax.dynamic_slice_in_dim(dec_bias, s * share, share)
    error = (carry + dec_own - activations.astype(F32)).astype(BF)

    ring_e = [error]
    for t in range(1, nz):
        ring_e.append(along_ring(ring_e[-1]))
    run(plan_e, [{0: [e]} for e in ring_e])
    own_terms = [results["D"][t] for t in range(nz)]
    sib_terms = [sib_terms[t] for t in range(nz)]

    codes = jnp.stack(codes)
    which = pick(jnp.concatenate([codes, to_sibling(codes)]))[0][0]
    terms = own_terms + sib_terms
    nt = len(terms)
    meta = jnp.concatenate([which, place])
    grad_w, grad_b = pl.pallas_call(
        functools.partial(sum_kernel, nt),
        grid_spec=pltpu.PrefetchScalarGridSpec(
            num_scalar_prefetch=1,
            grid=(ns, 2),
            in_specs=[pl.BlockSpec((SPAN // 2, fw), lambda j, k, m: (k, j))] * nt
            + [pl.BlockSpec((EXTRA, SPAN), lambda j, k, m: (SPAN // EXTRA, 0))] * nt,
            out_specs=[
                pl.BlockSpec((own_blocks, SPAN // 2, fw), lambda j, k, m: (0, k, m[nt + j])),
                pl.BlockSpec((own_blocks, 1, SPAN), lambda j, k, m: (0, 0, 0)),
            ],
        ),
        out_shape=[
            jax.ShapeDtypeStruct((own_blocks, SPAN, width), F32),
            jax.ShapeDtypeStruct((own_blocks, 1, SPAN), F32),
        ],
        compiler_params=pltpu.CompilerParams(vmem_limit_bytes=VMEM_LIMIT),
        cost_estimate=pl.CostEstimate(
            flops=nt * SPAN * width,
            bytes_accessed=2 * nt * SPAN * width + 4 * own_blocks * SPAN * width,
            transcendentals=0,
        ),
    )(meta, *terms, *terms)
    grad_w = grad_w.reshape(own_blocks * SPAN, width)
    if not aligned:
        grad_w = grad_w.reshape(-1, nd, share)[:, order].reshape(-1, width)
    return error, grad_w, grad_b.reshape(own_blocks * SPAN)


def solution(mesh):
    in_specs = (
        P("dp", "dict"),
        P(("dict", "dp"), None),
        P(("dict", "dp")),
        P(),
        P("dp", None, None),
    )
    out_specs = (P("dp", "dict"), P(("dict", "dp"), None), P(("dict", "dp")))
    return jax.shard_map(shards, mesh=mesh, in_specs=in_specs, out_specs=out_specs, check_vma=False)
```

```python
import functools

import jax
import jax.numpy as jnp
from jax import lax
from jax.experimental import pallas as pl
from jax.experimental.pallas import tpu as pltpu
from jax.sharding import PartitionSpec as P

SPAN = 128
EXTRA = 16
VMEM_LIMIT = 30 * 1024 * 1024
PLAN_X = (
    "a010", "a110 S0", "a020 a121", "k1", "k0", "a210", "r11", "a310", "a220 a321",
    "k2", "h1", "r22", "k3", "r32", "r21", "r31", "r02", "r01",
)
PLAN_E = (
    "a010", "a022", "a110", "g1", "a310", "d0", "a210 D0", "d1", "a322", "a222 D1", "d3", "d2",
)
DEPTH = 2
BF = jnp.bfloat16
F32 = jnp.float32


def hop_bit(slot, half):
    return 1 << (slot.bit_length() - 1) if half == 0 else slot & -slot


class Steps:
    def __init__(self):
        self.done = []

    def send(self, items, after=(), depth=DEPTH):
        held = list(after) + (self.done[-depth] if len(self.done) >= depth > 0 else [])
        out = []
        for x, bit in items:
            if held:
                x = lax.optimization_barrier((x, *held))[0]
            out.append(over_dict(x, bit))
        self.done.append(out)
        return out


def over_dict(x, bit):
    n = lax.axis_size("dict")
    return lax.ppermute(x, "dict", [(i, i ^ bit) for i in range(n)])


def to_sibling(x):
    n = lax.axis_size("dp")
    return lax.ppermute(x, "dp", [(i, i ^ 1) for i in range(n)])


def along_ring(x, hops=1):
    n = lax.axis_size("dp")
    return lax.ppermute(x, "dp", [(i, (i + 2 * hops) % n) for i in range(n)])


def gather_level(slots, count, mode):
    n = lax.axis_size("dict")
    items, keys = [], []
    for slot in range(1, n):
        if slot.bit_count() != count:
            continue
        if count == 1 or mode < 2:
            bit = hop_bit(slot, mode % 2)
            source = slots[slot ^ bit]
            items.append((source[0] if len(source) == 1 else jnp.concatenate(source, axis=0), bit))
            keys.append((slot, 0))
        else:
            for h in (0, 1):
                bit = hop_bit(slot, h)
                source = slots[slot ^ bit]
                if len(source) == 1:
                    half = source[0].shape[0] // 2
                    items.append((source[0][h * half : (h + 1) * half], bit))
                else:
                    items.append((source[h], bit))
                keys.append((slot, h))
    return items, keys


def gather_store(slots, keys, got):
    for (slot, _), x in zip(keys, got):
        slots.setdefault(slot, []).append(x)


def scatter_level(acc, count):
    n = lax.axis_size("dict")
    items, keys = [], []
    for slot in range(1, n):
        if slot.bit_count() != count:
            continue
        if len(acc[slot]) == 1:
            bit = slot
            items.append((acc[slot][0].astype(BF), bit))
            keys.append((0, None))
        else:
            for h in (0, 1):
                bit = hop_bit(slot, h)
                items.append((acc[slot][h].astype(BF), bit))
                keys.append((slot ^ bit, h))
    return items, keys


def scatter_store(acc, keys, got):
    for (slot, h), x in zip(keys, got):
        x = x.astype(F32)
        if h is None:
            acc[slot] = [acc[slot][0] + x]
        elif len(acc[slot]) == 2:
            acc[slot][h] = acc[slot][h] + x
        else:
            half = x.shape[0]
            grow = ((0, half), (0, 0)) if h == 0 else ((half, 0), (0, 0))
            acc[slot] = [acc[slot][0] + jnp.pad(x, grow)]


def nt_dot(a, b):
    return lax.dot_general(a, b, (((1,), (1,)), ((), ())), preferred_element_type=F32)


def fill_weights(w_refs, w_cat, fw):
    ns = len(w_refs) // 2
    for part in range(2):
        for j in range(ns):
            w_cat[part * SPAN : (part + 1) * SPAN, j * fw : (j + 1) * fw] = w_refs[part * ns + j][0]


def fill_rows(refs, layout, dst, fw, dec=None):
    for ref, (slot, row, count) in zip(refs, layout):
        cols = slice(slot * fw, (slot + 1) * fw)
        value = ref[...]
        if dec is not None:
            value = (value.astype(F32) - dec[:, cols]).astype(BF)
        dst[row : row + count, cols] = value


def fwd_kernel(layout, ns, fw, out_layout, meta, *refs):
    nx = len(layout)
    x_refs, refs = refs[:nx], refs[nx:]
    w_refs, refs = refs[: 2 * ns], refs[2 * ns :]
    dec, own_bias, sib_bias, lat_out = refs[:4]
    outs = refs[4 : 4 + len(out_layout)]
    xc, wc = refs[4 + len(out_layout) :]
    fill_weights(w_refs, wc, fw)
    fill_rows(x_refs, layout, xc, fw, dec)
    preact = nt_dot(xc[...], wc[...])
    biases = (own_bias[0].astype(F32), sib_bias[0].astype(F32))
    tokens = preact.shape[0]
    for tb in range(tokens // SPAN):
        for part in range(2):
            cell = (slice(tb * SPAN, (tb + 1) * SPAN), slice(part * SPAN, (part + 1) * SPAN))
            named = jnp.full((SPAN, SPAN), meta[2 + 2 * tb + part], jnp.int32) > 0
            lat_out[cell] = jnp.where(named, jnp.maximum(preact[cell] + biases[part], 0.0), 0.0).astype(BF)
    lat = lat_out[...]
    for j in range(ns):
        recon = jnp.dot(lat, wc[:, j * fw : (j + 1) * fw], preferred_element_type=F32)
        for out, (slot, row, count) in zip(outs, out_layout):
            if slot == j:
                out[...] = recon[row : row + count].astype(out.dtype)


def bwd_kernel(x_layout, e_layout, ns, fw, meta, *refs):
    nx, ne = len(x_layout), len(e_layout)
    x_refs, refs = refs[:nx], refs[nx:]
    e_refs, refs = refs[:ne], refs[ne:]
    w_refs, refs = refs[: 2 * ns], refs[2 * ns :]
    dec, lat_ref, own_out, sib_out, xc, ec, wc = refs
    fill_weights(w_refs, wc, fw)
    fill_rows(e_refs, e_layout, ec, fw)
    fill_rows(x_refs, x_layout, xc, fw, dec)
    lat = lat_ref[...]
    back = nt_dot(ec[...], wc[...])
    slope = jnp.where(lat > 0, back, 0.0).astype(BF)
    bias = jnp.sum(slope.astype(F32), axis=0, keepdims=True).astype(BF)
    lat_t, slope_t = lat.T, slope.T
    for part, out in enumerate((own_out, sib_out)):
        out[SPAN:, :SPAN] = jnp.broadcast_to(bias[:, part * SPAN : (part + 1) * SPAN], (EXTRA, SPAN))
    for j in range(ns):
        cols = slice(j * fw, (j + 1) * fw)
        grad = jnp.dot(lat_t, ec[:, cols], preferred_element_type=F32) + jnp.dot(
            slope_t, xc[:, cols], preferred_element_type=F32
        )
        own_out[:SPAN, cols] = grad[:SPAN].astype(BF)
        sib_out[:SPAN, cols] = grad[SPAN:].astype(BF)


def sum_kernel(terms, meta, *refs):
    w_refs, b_refs = refs[:terms], refs[terms : 2 * terms]
    w_out, b_out = refs[2 * terms :]
    w_out[...] = jnp.zeros_like(w_out)
    for i in range(terms):
        block = meta[i]

        @pl.when(block >= 0)
        def _(i=i, block=block):
            w_out[block] += w_refs[i][...].astype(F32)

    @pl.when((pl.program_id(0) == 0) & (pl.program_id(1) == 0))
    def _():
        b_out[...] = jnp.zeros_like(b_out)
        for i in range(terms):
            block = meta[i]

            @pl.when(block >= 0)
            def _(i=i, block=block):
                b_out[block] += b_refs[i][0:1].astype(F32)


def shards(activations, dictionary, enc_bias, dec_bias, block_codes):
    nd, npar = lax.axis_size("dict"), lax.axis_size("dp")
    nz = npar // 2
    s, d = lax.axis_index("dict"), lax.axis_index("dp")
    tokens, share = activations.shape
    width = dictionary.shape[1]
    own_blocks = dictionary.shape[0] // SPAN
    shard_blocks = own_blocks * npar
    ntb = block_codes.shape[0]
    aligned = share % SPAN == 0
    ns, fw = (nd, share) if aligned else (1, width)

    mine = lax.dynamic_index_in_dim(block_codes, s, axis=1, keepdims=False)
    everyone = lax.all_to_all(jnp.broadcast_to(mine, (npar, *mine.shape)), "dp", 0, 0)
    codes = [everyone[(d + 2 * (nz - t)) % npar] for t in range(nz)]
    ring_x = [activations]
    for t in range(1, nz):
        ring_x.append(along_ring(ring_x[-1]))

    def pick(codes):
        filled = codes >= 0
        local = codes - s * shard_blocks
        owner = jnp.where(filled, local // own_blocks, -1)
        inner = jnp.where(filled, local % own_blocks, -1)
        match = owner == jnp.stack([d, d ^ 1])[:, None, None, None]
        picked = jnp.max(jnp.where(match, inner, -1), axis=(2, 3))
        return picked, jnp.any(match, axis=3).astype(jnp.int32)

    order = s ^ jnp.arange(nd, dtype=jnp.int32)
    dec_rel = dec_bias.reshape(nd, share)[order].reshape(1, width)
    table = dictionary
    if not aligned:
        table = table.reshape(-1, nd, share)[:, order].reshape(-1, width)
    own_w = table.reshape(own_blocks, SPAN, width)
    sib_w = to_sibling(own_w)
    own_b = enc_bias.reshape(own_blocks, 1, SPAN)
    sib_b = to_sibling(own_b)
    place = order if aligned else jnp.zeros((1,), jnp.int32)

    def metas_of(codes):
        picked, named = pick(jnp.stack(codes))
        n = len(codes)
        metas = jnp.concatenate(
            [
                jnp.maximum(picked, 0).T,
                named.transpose(1, 2, 0).reshape(n, 2 * ntb),
                jnp.broadcast_to(place, (n, place.shape[0])),
            ],
            axis=1,
        )
        return [metas[t] for t in range(n)]

    metas = metas_of(codes)
    base = 2 + 2 * ntb

    def w_specs():
        return [
            pl.BlockSpec((1, SPAN, fw), lambda i, m, part=part, j=j: (m[part], 0, m[base + j]))
            for part in range(2)
            for j in range(ns)
        ]

    def b_specs():
        return [
            pl.BlockSpec((1, 1, SPAN), lambda i, m, part=part: (m[part], 0, 0)) for part in range(2)
        ]

    def whole(shape):
        return pl.BlockSpec(shape, lambda i, m: (0,) * len(shape))

    def flatten(slots):
        if not aligned:
            slots = [[jnp.concatenate(q, axis=0) if len(q) > 1 else q[0]] for q in slots]
            return [jnp.concatenate([q[0] for q in slots], axis=1)], [(0, 0, tokens)]
        pieces, layout = [], []
        for j, slot in enumerate(slots):
            row = 0
            for piece in slot:
                pieces.append(piece)
                layout.append((j, row, piece.shape[0]))
                row += piece.shape[0]
        return pieces, layout

    half = tokens // 2

    def forward(slots, meta, last):
        pieces, layout = flatten(slots)
        if aligned:
            out_layout, dtypes = [], []
            for j in range(nd):
                if j.bit_count() < 2:
                    out_layout.append((j, 0, tokens))
                    dtypes.append(F32)
                else:
                    out_layout += [(j, 0, half), (j, half, half)]
                    dtypes += [last if j == nd - 1 else F32] * 2
        else:
            out_layout, dtypes = [(0, 0, tokens)], [F32]
        res = pl.pallas_call(
            functools.partial(fwd_kernel, layout, ns, fw, out_layout),
            grid_spec=pltpu.PrefetchScalarGridSpec(
                num_scalar_prefetch=1,
                grid=(1,),
                in_specs=[whole(p.shape) for p in pieces]
                + w_specs()
                + [whole((1, width))]
                + b_specs(),
                out_specs=[whole((tokens, 2 * SPAN))] + [whole((c, fw)) for _, _, c in out_layout],
                scratch_shapes=[pltpu.VMEM((tokens, width), BF), pltpu.VMEM((2 * SPAN, width), BF)],
            ),
            out_shape=[jax.ShapeDtypeStruct((tokens, 2 * SPAN), BF)]
            + [jax.ShapeDtypeStruct((c, fw), t) for (_, _, c), t in zip(out_layout, dtypes)],
            compiler_params=pltpu.CompilerParams(vmem_limit_bytes=VMEM_LIMIT),
            cost_estimate=pl.CostEstimate(
                flops=8 * tokens * SPAN * width, bytes_accessed=8 * tokens * width, transcendentals=0
            ),
        )(meta, *pieces, *([own_w] * ns), *([sib_w] * ns), dec_rel, own_b, sib_b)
        lat, outs = res[0], res[1:]
        if aligned:
            acc = {}
            for out, (j, _, _) in zip(outs, out_layout):
                acc.setdefault(j, []).append(out)
            return lat, acc
        full = outs[0].reshape(tokens, nd, share)
        split = {j: [full[:, j]] if j.bit_count() < 2 else [full[:half, j], full[half:, j]] for j in range(nd)}
        return lat, split

    def backward(x_slots, e_slots, lat, meta):
        xp, xl = flatten(x_slots)
        ep, el = flatten(e_slots)
        rows = SPAN + EXTRA
        return pl.pallas_call(
            functools.partial(bwd_kernel, xl, el, ns, fw),
            grid_spec=pltpu.PrefetchScalarGridSpec(
                num_scalar_prefetch=1,
                grid=(1,),
                in_specs=[whole(p.shape) for p in xp + ep]
                + w_specs()
                + [whole((1, width)), whole((tokens, 2 * SPAN))],
                out_specs=[whole((rows, width))] * 2,
                scratch_shapes=[
                    pltpu.VMEM((tokens, width), BF),
                    pltpu.VMEM((tokens, width), BF),
                    pltpu.VMEM((2 * SPAN, width), BF),
                ],
            ),
            out_shape=[jax.ShapeDtypeStruct((rows, width), BF)] * 2,
            compiler_params=pltpu.CompilerParams(vmem_limit_bytes=VMEM_LIMIT),
            cost_estimate=pl.CostEstimate(
                flops=12 * tokens * SPAN * width, bytes_accessed=10 * tokens * width, transcendentals=0
            ),
        )(meta, *xp, *ep, *([own_w] * ns), *([sib_w] * ns), dec_rel, lat)

    levels = nd.bit_length() - 1
    paired = nd == 4 and nz == 4
    results = {"K": {}, "D": {}, "C": {t: c for t, c in enumerate(codes)}}
    accs, sib_terms = {}, {}

    def run(plan, slots):
        steps = Steps()
        fed = {int(w[1]) for line in plan for w in line.split() if w[0] == "h"}
        for line in plan:
            words = line.split()
            after, depth = [], DEPTH if paired else 0
            for w in words:
                if w[0] == "S":
                    after += steps.done[int(w[1:])]
                elif w[0] in results:
                    after.append(results[w[0]][int(w[1:])])
                elif w[0] == "/":
                    depth = int(w[1:])
            hold = lambda x: lax.optimization_barrier((x, *after))[0] if after else x
            items, stores = [], []
            for w in words:
                if w[0] not in "arkdgh":
                    continue
                t = int(w[1])
                if w[0] == "a":
                    more, keys = gather_level(slots[t], int(w[2]), int(w[3]))
                    stores.append((gather_store, slots[t], keys, len(items)))
                    items += more
                elif w[0] == "r":
                    more, keys = scatter_level(accs[t], int(w[2]))
                    stores.append((scatter_store, accs[t], keys, len(items)))
                    items += more
                elif w[0] == "k":
                    last = F32 if t - 1 in fed else BF
                    lat, accs[t] = forward([slots[t][j] for j in range(nd)], hold(metas[t]), last)
                    results["K"][t] = lat
                elif w[0] == "d":
                    results["D"][t], theirs = backward(
                        [x_slots[t][j] for j in range(nd)],
                        [slots[t][j] for j in range(nd)],
                        results["K"][t],
                        hold(metas[t]),
                    )
                    sib_terms[t] = to_sibling(theirs)
                elif w[0] == "g":
                    slots[t][nd - 1] = [along_ring(hold(x)) for x in slots[t - 1][nd - 1]]
                elif w[0] == "h":
                    moved = [along_ring(hold(x.astype(BF))) for x in accs[t].pop(nd - 1)]
                    accs[t + 1][nd - 1] = [x + y.astype(F32) for x, y in zip(accs[t + 1][nd - 1], moved)]
            if items:
                got = steps.send(items, after, depth)
                for store, where, keys, at in stores:
                    store(where, keys, got[at : at + len(keys)])

    ring_order = list(range(1, nz)) + [0]
    plan_x, plan_e = PLAN_X, PLAN_E
    if not paired:
        plan_x, plan_e = [], []
        for t in range(nz):
            gather = [f"a{t}{c}2" for c in range(1, levels + 1)]
            plan_x += gather + [f"k{t}"]
            plan_e += gather + [f"d{t}"]
        plan_x += [f"r{t}{c}" for t in ring_order for c in range(levels, 0, -1)]
    x_slots = [{0: [x]} for x in ring_x]
    run(plan_x, x_slots)
    carry = None
    for t in ring_order:
        total = accs[t][0][0]
        if carry is not None:
            total = total + along_ring(carry.astype(BF)).astype(F32)
        carry = total
    dec_own = lax.dynamic_slice_in_dim(dec_bias, s * share, share)
    error = (carry + dec_own - activations.astype(F32)).astype(BF)

    ring_e = [error]
    for t in range(1, nz):
        if t == nz - 1 > 1:
            ring_e.append(along_ring(error, nz - 1))
        else:
            ring_e.append(along_ring(ring_e[-1]))
    codes = jnp.stack(codes)
    which = pick(jnp.concatenate([codes, to_sibling(codes)]))[0][0]
    metas[0], which = lax.optimization_barrier((metas[0], which))
    run(plan_e, [{0: [e]} for e in ring_e])
    own_terms = [results["D"][t] for t in range(nz)]
    sib_terms = [sib_terms[t] for t in range(nz)]

    terms = own_terms + sib_terms
    nt = len(terms)
    meta = jnp.concatenate([which, place])
    grad_w, grad_b = pl.pallas_call(
        functools.partial(sum_kernel, nt),
        grid_spec=pltpu.PrefetchScalarGridSpec(
            num_scalar_prefetch=1,
            grid=(ns, 2),
            in_specs=[pl.BlockSpec((SPAN // 2, fw), lambda j, k, m: (k, j))] * nt
            + [pl.BlockSpec((EXTRA, SPAN), lambda j, k, m: (SPAN // EXTRA, 0))] * nt,
            out_specs=[
                pl.BlockSpec((own_blocks, SPAN // 2, fw), lambda j, k, m: (0, k, m[nt + j])),
                pl.BlockSpec((own_blocks, 1, SPAN), lambda j, k, m: (0, 0, 0)),
            ],
        ),
        out_shape=[
            jax.ShapeDtypeStruct((own_blocks, SPAN, width), F32),
            jax.ShapeDtypeStruct((own_blocks, 1, SPAN), F32),
        ],
        compiler_params=pltpu.CompilerParams(vmem_limit_bytes=VMEM_LIMIT),
        cost_estimate=pl.CostEstimate(
            flops=nt * SPAN * width,
            bytes_accessed=2 * nt * SPAN * width + 4 * own_blocks * SPAN * width,
            transcendentals=0,
        ),
    )(meta, *terms, *terms)
    grad_w = grad_w.reshape(own_blocks * SPAN, width)
    if not aligned:
        grad_w = grad_w.reshape(-1, nd, share)[:, order].reshape(-1, width)
    return error, grad_w, grad_b.reshape(own_blocks * SPAN)


def solution(mesh):
    in_specs = (
        P("dp", "dict"),
        P(("dict", "dp"), None),
        P(("dict", "dp")),
        P(),
        P("dp", None, None),
    )
    out_specs = (P("dp", "dict"), P(("dict", "dp"), None), P(("dict", "dp")))
    return jax.shard_map(shards, mesh=mesh, in_specs=in_specs, out_specs=out_specs, check_vma=False)
```
